32 devices in a mesh: row: 4 (over z), col: 8 (over y, x, core).
Axes of the slice: x: 2, y: 2, z: 4, core: 2. Of those that a mesh axis runs over, the one named last changes fastest.
Arguments:
- finetune: bfloat16 [2048, 53248], P('row', 'col'), may hold values from -6 to 6
- base_rows: bfloat16 [4096, 53248], P(('row', 'col')), may hold values from -6 to 6
- test_matrix: bfloat16 [256, 53248], P(None, 'col'), may hold values from -0.02734375 to 0.02734375
- base_lengths: int32 [32], replicated, may hold values from 0 to 128, as said below
Outputs:
- basis_out: float32 [2048, 256], P(('row', 'col'))
- coefficients: float32 [256, 53248], P('row', 'col')
The draws below stay inside these ranges and needn't reach their ends.
Inputs may be any that keep to these rules, and one draw needn't show every extreme that they name: Number devices d = row index * 8 + col index. Devices 2m and 2m+1 hold together slab rows m * 128 to m * 128 + 127: device 2m the first base_lengths[2m] of them, device 2m+1 the rest, each from its slot 0 on, so entries 2m and 2m+1 sum to 128. In every draw some device holds 128 rows and some none. Slots past a device's count hold no slab data.
All inputs are finite; a program needn't handle non-finite values.
Results may differ from the reference program's by a relative error of at most 0.014.
Values may be sent and summed in bfloat16 or wider, within the bound.
A program may use at most 128 MiB of HBM per device.

```python
import math
import jax
import jax.numpy as jnp
from jax import lax

C = 53248
K = 256
SHARDS = 32
CAP = 128
ROWS = 2048


def draw_base_lengths(key, part):
    pair_count = SHARDS // 2
    key_first, key_full, key_empty = jax.random.split(jax.random.fold_in(key, 7), 3)
    first_counts = jax.random.randint(key_first, (pair_count,), 0, CAP + 1)
    full_pair = jax.random.randint(key_full, (), 0, pair_count)
    empty_pair = (full_pair + 1 + jax.random.randint(key_empty, (), 0, pair_count - 1)) % pair_count
    pair_ids = jnp.arange(pair_count)
    first_counts = jnp.where(pair_ids == full_pair, CAP, first_counts)
    first_counts = jnp.where(pair_ids == empty_pair, 0, first_counts)
    return jnp.stack([first_counts, CAP - first_counts], axis=1).reshape(SHARDS).astype(jnp.int32)


def block_scale(own_key, extent, shards, low, largest):
    gain = 1.0
    for axis_at, blocks in shards:
        draws = jax.random.uniform(jax.random.fold_in(jax.random.fold_in(own_key, 6), axis_at), (blocks,), jnp.float32, low / len(shards), largest / len(shards))
        gain = gain * jnp.repeat(jnp.exp(draws), extent[axis_at] // blocks).reshape((-1,) + (1,) * (len(extent) - 1 - axis_at))
    return gain


def noise(rng, dims, width, limit, cuts=(), kind=jnp.bfloat16):
    result = width * jax.random.normal(rng, dims, jnp.float32)
    if cuts:
        result = result * block_scale(rng, dims, cuts, -0.22, 0.18)
    return jnp.clip(result, -limit, limit).astype(kind)


def setup_inputs(seed: int = 0) -> dict:
    seeds = jax.random.split(jax.random.key(seed), 5)
    return {
        "finetune": noise(seeds[0], (ROWS, C), 1.0, 6.0, ((0, 4), (1, 8))),
        "base_rows": noise(seeds[1], (SHARDS * CAP, C), 1.0, 6.0, ((0, 32),)),
        "test_matrix": noise(seeds[2], (K, C), C ** -0.5, 0.02734375, ((1, 8),)),
        "base_lengths": draw_base_lengths(jax.random.fold_in(seeds[4], 71), 0),
    }


def compose(first_half, second_half, first_count):
    capacity = first_half.shape[0]
    row_ids = jnp.arange(capacity)[:, None]
    padded = jnp.concatenate([jnp.zeros_like(second_half), second_half], axis=0)
    shifted = lax.dynamic_slice_in_dim(padded, (capacity - first_count).astype(jnp.int32), capacity, 0)
    return jnp.where(row_ids < first_count, first_half, shifted)

def orthonormal(sketched):
    gram_matrix = jnp.dot(sketched.T, sketched, precision=lax.Precision.HIGHEST)
    factor = jnp.linalg.cholesky(gram_matrix)
    identity = jnp.eye(gram_matrix.shape[0], dtype=gram_matrix.dtype)
    inverse = lax.linalg.triangular_solve(factor, identity, left_side=True, lower=True)
    return jnp.dot(sketched, inverse.T, precision=lax.Precision.HIGHEST)

def reference(finetune, base_rows, test_matrix, base_lengths):
    pair_count = SHARDS // 2
    fine_pairs = finetune.reshape(pair_count, CAP, C)
    base_pairs = base_rows.reshape(pair_count, 2, CAP, C)
    firsts = base_lengths.reshape(pair_count, 2)[:, 0]
    pair_ids = jnp.arange(pair_count).astype(jnp.int32)

    def delta_block(pair_index):
        merged = compose(base_pairs[pair_index, 0], base_pairs[pair_index, 1], firsts[pair_index])
        return fine_pairs[pair_index].astype(jnp.float32) - merged.astype(jnp.float32)

    def sketch(right_side):
        right_wide = right_side.astype(jnp.float32)
        blocks = lax.map(lambda pair_index: jnp.dot(delta_block(pair_index), right_wide.T, precision=lax.Precision.HIGHEST), pair_ids)
        return blocks.reshape(ROWS, K)

    def project(narrow_basis):
        wide_basis = narrow_basis.astype(jnp.float32).reshape(pair_count, CAP, K)

        def advance(running, pair_index):
            return (running + jnp.dot(wide_basis[pair_index].T, delta_block(pair_index), precision=lax.Precision.HIGHEST), None)
        running, unused = lax.scan(advance, jnp.zeros((K, C), jnp.float32), pair_ids)
        return running
    first_basis = orthonormal(sketch(test_matrix))
    projection = project(first_basis.astype(jnp.bfloat16)).astype(jnp.bfloat16)
    second_basis = orthonormal(sketch(projection))
    basis_out = second_basis * math.sqrt(ROWS)
    coefficients = project(second_basis.astype(jnp.bfloat16))
    return (basis_out, coefficients)
```

```python
import functools
import math

import jax
import jax.numpy as jnp
from jax import lax
from jax.experimental import pallas as pl
from jax.experimental.pallas import tpu as pltpu
from jax.sharding import PartitionSpec as P

MESH = pl.DeviceIdType.MESH
HIGHEST = lax.Precision.HIGHEST
VMEM_LIMIT = 58 * 1024 * 1024


def flip(index, mask, count):
    if count & (count - 1):
        raise ValueError("count")
    result, bit = 0, 1
    while bit < count:
        digit = lax.rem(lax.div(index, bit), 2)
        result = result + bit * ((1 - digit) if mask & bit else digit)
        bit *= 2
    return result


def column_tile(width):
    lanes = width // 128
    return 128 * max(d for d in range(1, 9) if lanes % d == 0)


def gather_kernel(
    chips, select, base, fine, test, delta, sketch,
    mine, other, landed, work,
    mine_sem, pair_send, pair_recv, send_sem, recv_sem, fine_sem, delta_sem,
):
    row = lax.axis_index("row")
    col = lax.axis_index("col")
    chip = lax.div(col, 2)
    core = lax.rem(col, 2)
    rows, width = mine.shape[1], mine.shape[2]
    tile = column_tile(width)
    partner = (row, 2 * chip + (1 - core))

    barrier = pltpu.get_barrier_semaphore()
    pl.semaphore_signal(barrier, inc=1, device_id=partner, device_id_type=MESH)
    for o in range(1, chips):
        pl.semaphore_signal(
            barrier, inc=1, device_id=(row, 2 * flip(chip, o, chips) + core), device_id_type=MESH
        )
    pl.semaphore_wait(barrier, chips)

    order = list(range(chips - 1, -1, -1))
    pair, local = {}, {}
    for o in order:
        block = flip(chip, o, chips)
        away = pl.ds(pl.multiple_of((2 * block + (1 - core)) * width, 128), width)
        keep = pl.ds(pl.multiple_of((2 * block + core) * width, 128), width)
        pair[o] = pltpu.make_async_remote_copy(
            src_ref=base.at[:, away], dst_ref=other.at[o],
            send_sem=pair_send.at[o], recv_sem=pair_recv.at[o],
            device_id=partner, device_id_type=MESH,
        )
        pair[o].start()
        local[o] = pltpu.make_async_copy(base.at[:, keep], mine.at[o], mine_sem.at[o])
        local[o].start()
    loads = {}
    for o in order:
        block = flip(chip, o, chips)
        here = pl.ds(pl.multiple_of(block * rows, rows), rows)
        loads[o] = pltpu.make_async_copy(fine.at[here, :], work.at[o], fine_sem.at[o])
        loads[o].start()

    sends = {}
    for o in order:
        local[o].wait()
        pair[o].wait_recv()

        @pl.loop(0, width // tile)
        def compose(step):
            at = pl.ds(pl.multiple_of(step * tile, 128), tile)
            merged = jnp.dot(select[0], mine[o, :, at], preferred_element_type=jnp.float32)
            merged += jnp.dot(select[1], other[o, :, at], preferred_element_type=jnp.float32)
            mine[o, :, at] = merged.astype(jnp.bfloat16)

        if o:
            sends[o] = pltpu.make_async_remote_copy(
                src_ref=mine.at[o], dst_ref=landed.at[o],
                send_sem=send_sem.at[o], recv_sem=recv_sem.at[o],
                device_id=(row, 2 * flip(chip, o, chips) + core), device_id_type=MESH,
            )
            sends[o].start()

    stores = []
    for o in [0] + order[:-1]:
        block = flip(chip, o, chips)
        here = pl.ds(pl.multiple_of(block * rows, rows), rows)
        if o:
            sends[o].wait_recv()
        loads[o].wait()
        source = landed if o else mine

        def difference(step, total):
            at = pl.ds(pl.multiple_of(step * tile, 128), tile)
            value = work[o, :, at].astype(jnp.float32) - source[o, :, at].astype(jnp.float32)
            value = value.astype(jnp.bfloat16)
            work[o, :, at] = value
            return total + lax.dot_general(
                value, test[:, at], (((1,), (1,)), ((), ())), preferred_element_type=jnp.float32
            )

        total = lax.fori_loop(
            0, width // tile, difference, jnp.zeros((rows, test.shape[0]), jnp.float32)
        )
        sketch[here, :] = total
        store = pltpu.make_async_copy(work.at[o], delta.at[here, :], delta_sem.at[o])
        store.start()
        stores.append(store)
    for store in stores:
        store.wait()
    for o in order:
        pair[o].wait_send()
        if o:
            sends[o].wait_send()


def sum_kernel(
    col_count, row_count, partial, full, gram,
    arrived, local_gram, crossed,
    a_send, a_recv, b_send, b_recv, c_send, c_recv, d_send, d_recv,
):
    row = lax.axis_index("row")
    col = lax.axis_index("col")
    own_rows = arrived.shape[1]
    gram_rows = crossed.shape[1]

    def peer(o):
        return lax.rem(col + o, col_count)

    def above(o):
        return lax.rem(row + o, row_count)

    barrier = pltpu.get_barrier_semaphore()
    for o in range(1, col_count):
        pl.semaphore_signal(barrier, inc=1, device_id=(row, peer(o)), device_id_type=MESH)
    for o in range(1, row_count):
        pl.semaphore_signal(barrier, inc=1, device_id=(above(o), col), device_id_type=MESH)
    pl.semaphore_wait(barrier, col_count + row_count - 2)

    own = pl.ds(pl.multiple_of(col * own_rows, own_rows), own_rows)
    strip = pl.ds(pl.multiple_of(col * gram_rows, gram_rows), gram_rows)

    def copy(source, target, send, recv, o, device):
        made = pltpu.make_async_remote_copy(
            src_ref=source, dst_ref=target, send_sem=send.at[o], recv_sem=recv.at[o],
            device_id=device, device_id_type=MESH,
        )
        made.start()
        return made

    first = []
    for o in range(1, col_count):
        theirs = pl.ds(pl.multiple_of(peer(o) * own_rows, own_rows), own_rows)
        first.append(
            copy(partial.at[theirs, :], arrived.at[o], a_send, a_recv, o, (row, peer(o)))
        )
    total = partial[own, :]
    for o in range(1, col_count):
        first[o - 1].wait_recv()
        total = total + arrived[o]
    full[own, :] = total
    second = [
        copy(full.at[own, :], full.at[own, :], b_send, b_recv, o, (row, peer(o)))
        for o in range(1, col_count)
    ]
    for made in second:
        made.wait_recv()
    local_gram[...] = lax.dot_general(
        full[...], full[...], (((0,), (0,)), ((), ())),
        precision=HIGHEST, preferred_element_type=jnp.float32,
    )
    third = [
        copy(local_gram.at[strip, :], crossed.at[o], c_send, c_recv, o, (above(o), col))
        for o in range(1, row_count)
    ]
    total = local_gram[strip, :]
    for o in range(1, row_count):
        third[o - 1].wait_recv()
        total = total + crossed[o]
    gram[strip, :] = total
    fourth = [
        copy(gram.at[strip, :], gram.at[strip, :], d_send, d_recv, o, (row, peer(o)))
        for o in range(1, col_count)
    ]
    for made in fourth:
        made.wait_recv()
    for made in first + second + third + fourth:
        made.wait_send()


def factor_kernel(panel, scale, full, gram, own, narrow, basis, table):
    size = gram.shape[0]
    table[:, :size] = gram[...]
    row_ids = lax.broadcasted_iota(jnp.int32, (size, size), 0)
    column_ids = lax.broadcasted_iota(jnp.int32, (size, size), 1)
    table[:, size:] = (row_ids == column_ids).astype(jnp.float32)
    for start in range(0, size, panel):
        low = start // 128 * 128
        high = size + low + 128
        block = table[start:start + panel, low:high]
        ids = lax.broadcasted_iota(jnp.int32, (panel, 1), 0)
        pivots = jnp.ones((panel, 1), jnp.float32)
        for i in range(panel):
            at = start + i - low
            column = block[:, at:at + 1]
            line = block[i:i + 1, :]
            pivot = column[i:i + 1, :]
            pivots = jnp.where(ids == i, pivot, pivots)
            if i + 1 < panel:
                weight = jnp.where(ids > i, column * (1.0 / pivot), 0.0)
                block = block - weight * line
        block = block * (1.0 / jnp.sqrt(pivots))
        table[start:start + panel, low:high] = block
        end = start + panel
        if end < size:
            update = lax.dot_general(
                block[:, :size - low], block, (((0,), (0,)), ((), ())),
                precision=HIGHEST, preferred_element_type=jnp.float32,
            )
            table[end:, low:high] = table[end:, low:high] - update[end - low:, :]
    inverse = table[:, size:]
    inverse = jnp.where(column_ids <= row_ids, inverse, 0.0)

    def apply(rows):
        return lax.dot_general(
            rows, inverse, (((1,), (1,)), ((), ())),
            precision=HIGHEST, preferred_element_type=jnp.float32,
        )

    narrow[...] = apply(full[...]).astype(jnp.bfloat16)
    basis[...] = apply(own[...]) * scale


def vmem():
    return pl.BlockSpec(memory_space=pltpu.VMEM)


def anywhere():
    return pl.BlockSpec(memory_space=pl.ANY)


def gather(select, base_rows, finetune, test_matrix, chips):
    capacity = base_rows.shape[0]
    rows, width = finetune.shape
    sketch_size = test_matrix.shape[0]
    slots = pltpu.VMEM((chips, capacity, width), jnp.bfloat16)
    sems = pltpu.SemaphoreType.DMA((chips,))
    return pl.pallas_call(
        functools.partial(gather_kernel, chips),
        out_shape=(
            jax.ShapeDtypeStruct((rows, width), jnp.bfloat16),
            jax.ShapeDtypeStruct((rows, sketch_size), jnp.float32),
        ),
        in_specs=[vmem(), anywhere(), anywhere(), vmem()],
        out_specs=(anywhere(), vmem()),
        scratch_shapes=[slots] * 4 + [sems] * 7,
        compiler_params=pltpu.CompilerParams(
            collective_id=0, has_side_effects=True, vmem_limit_bytes=VMEM_LIMIT
        ),
        cost_estimate=pl.CostEstimate(
            flops=2 * rows * width * sketch_size, bytes_accessed=8 * rows * width, transcendentals=0
        ),
    )(select, base_rows, finetune, test_matrix)


def group_sums(partial, col_count, row_count, collective_id):
    rows, size = partial.shape
    col_sems = pltpu.SemaphoreType.DMA((col_count,))
    row_sems = pltpu.SemaphoreType.DMA((row_count,))
    return pl.pallas_call(
        functools.partial(sum_kernel, col_count, row_count),
        out_shape=(
            jax.ShapeDtypeStruct((rows, size), jnp.float32),
            jax.ShapeDtypeStruct((size, size), jnp.float32),
        ),
        in_specs=[vmem()],
        out_specs=(vmem(), vmem()),
        scratch_shapes=[
            pltpu.VMEM((col_count, rows // col_count, size), jnp.float32),
            pltpu.VMEM((size, size), jnp.float32),
            pltpu.VMEM((row_count, size // col_count, size), jnp.float32),
            col_sems, col_sems, col_sems, col_sems,
            row_sems, row_sems, col_sems, col_sems,
        ],
        compiler_params=pltpu.CompilerParams(
            collective_id=collective_id, has_side_effects=True, vmem_limit_bytes=VMEM_LIMIT
        ),
    )(partial)


def orthonormal(full, gram, own, scale):
    rows, size = full.shape
    return pl.pallas_call(
        functools.partial(factor_kernel, 32, scale),
        out_shape=(
            jax.ShapeDtypeStruct((rows, size), jnp.bfloat16),
            jax.ShapeDtypeStruct(own.shape, jnp.float32),
        ),
        in_specs=[vmem()] * 3,
        out_specs=(vmem(), vmem()),
        scratch_shapes=[pltpu.VMEM((size, 2 * size), jnp.float32)],
        compiler_params=pltpu.CompilerParams(vmem_limit_bytes=VMEM_LIMIT),
    )(full, gram, own)


def per_device(finetune, base_rows, test_matrix, base_lengths):
    col_count = lax.axis_size("col")
    row_count = lax.axis_size("row")
    col = lax.axis_index("col")
    row = lax.axis_index("row")
    capacity = base_rows.shape[0]
    chips = col_count // 2
    group = finetune.shape[0]
    total_rows = group * row_count
    own_rows = group // col_count

    first_count = lax.dynamic_index_in_dim(
        base_lengths, row * col_count + col // 2 * 2, 0, keepdims=False
    )
    slab_row = jnp.arange(capacity)[:, None]
    slot = jnp.arange(capacity)[None, :]
    from_first = (slab_row == slot) & (slab_row < first_count)
    from_second = slab_row - first_count == slot
    is_first = col % 2 == 0
    select = jnp.stack(
        [jnp.where(is_first, from_first, from_second), jnp.where(is_first, from_second, from_first)]
    ).astype(jnp.bfloat16)

    delta, partial = gather(select, base_rows, finetune, test_matrix, chips)
    for sweep in range(2):
        full, gram = group_sums(partial, col_count, row_count, 1 + sweep)
        own = lax.dynamic_slice_in_dim(full, col * own_rows, own_rows, 0)
        narrow, basis = orthonormal(full, gram, own, math.sqrt(total_rows))
        projected = lax.dot_general(
            narrow, delta, (((0,), (0,)), ((), ())), preferred_element_type=jnp.float32
        ).astype(jnp.bfloat16)
        if sweep == 0:
            right_side = lax.psum(projected, "row")
            partial = lax.dot_general(
                delta, right_side, (((1,), (1,)), ((), ())), preferred_element_type=jnp.float32
            )
    coefficients = lax.psum_scatter(
        projected, "row", scatter_dimension=0, tiled=True
    ).astype(jnp.float32)
    return (basis, coefficients)


def solution(mesh):
    return jax.shard_map(
        per_device,
        mesh=mesh,
        in_specs=(P("row", "col"), P(("row", "col"), None), P(None, "col"), P()),
        out_specs=(P(("row", "col"), None), P("row", "col")),
        check_vma=False,
    )
```

```python
import functools
import math

import jax
import jax.numpy as jnp
from jax import lax
from jax.experimental import pallas as pl
from jax.experimental.pallas import tpu as pltpu
from jax.sharding import PartitionSpec as P

MESH = pl.DeviceIdType.MESH
HIGHEST = lax.Precision.HIGHEST
VMEM_LIMIT = 58 * 1024 * 1024


def flip(index, mask, count):
    if count & (count - 1):
        raise ValueError("count")
    result, bit = 0, 1
    while bit < count:
        digit = lax.rem(lax.div(index, bit), 2)
        result = result + bit * ((1 - digit) if mask & bit else digit)
        bit *= 2
    return result


def column_tile(width):
    lanes = width // 128
    return 128 * max(d for d in range(1, 9) if lanes % d == 0)


def gather_kernel(
    chips, select, base, fine, test, delta, sketch,
    mine, other, landed, work,
    mine_sem, pair_send, pair_recv, send_sem, recv_sem, fine_sem, delta_sem,
):
    row = lax.axis_index("row")
    col = lax.axis_index("col")
    chip = lax.div(col, 2)
    core = lax.rem(col, 2)
    rows, width = mine.shape[1], mine.shape[2]
    pieces = mine_sem.shape[1]
    tile = width // pieces
    partner = (row, 2 * chip + (1 - core))

    barrier = pltpu.get_barrier_semaphore()
    pl.semaphore_signal(barrier, inc=1, device_id=partner, device_id_type=MESH)
    for o in range(1, chips):
        pl.semaphore_signal(
            barrier, inc=1, device_id=(row, 2 * flip(chip, o, chips) + core), device_id_type=MESH
        )
    pl.semaphore_wait(barrier, chips)

    far = list(range(chips - 1, 0, -1))

    def columns(q):
        return pl.ds(pl.multiple_of(q * tile, 128), tile)

    def rows_of(o):
        return pl.ds(pl.multiple_of(flip(chip, o, chips) * rows, rows), rows)

    def source(o, q, side):
        start = (2 * flip(chip, o, chips) + side) * width + q * tile
        return base.at[:, pl.ds(pl.multiple_of(start, 128), tile)]

    def pair(o, q):
        return pltpu.make_async_remote_copy(
            src_ref=source(o, q, 1 - core), dst_ref=other.at[o, :, columns(q)],
            send_sem=pair_send.at[o, q], recv_sem=pair_recv.at[o, q],
            device_id=partner, device_id_type=MESH,
        )

    def keep(o, q):
        return pltpu.make_async_copy(
            source(o, q, core), mine.at[o, :, columns(q)], mine_sem.at[o, q]
        )

    def load(o):
        return pltpu.make_async_copy(fine.at[rows_of(o), :], work.at[o], fine_sem.at[o])

    def send(o, q):
        return pltpu.make_async_remote_copy(
            src_ref=mine.at[o, :, columns(q)], dst_ref=landed.at[o, :, columns(q)],
            send_sem=send_sem.at[o, q], recv_sem=recv_sem.at[o, q],
            device_id=(row, 2 * flip(chip, o, chips) + core), device_id_type=MESH,
        )

    def store(o, q):
        return pltpu.make_async_copy(
            work.at[o, :, columns(q)], delta.at[rows_of(o), columns(q)], delta_sem.at[o, q]
        )

    def compose(o, q):
        keep(o, q).wait()
        pair(o, q).wait_recv()
        merged = jnp.dot(
            select[0], mine[o, :, columns(q)], preferred_element_type=jnp.float32
        ) + jnp.dot(
            select[1], other[o, :, columns(q)], preferred_element_type=jnp.float32
        )
        mine[o, :, columns(q)] = merged.astype(jnp.bfloat16)

    def difference(o, q, composed):
        value = work[o, :, columns(q)].astype(jnp.float32)
        value = (value - composed[o, :, columns(q)].astype(jnp.float32)).astype(jnp.bfloat16)
        work[o, :, columns(q)] = value
        store(o, q).start()
        sketch[rows_of(o), :] += lax.dot_general(
            value, test[:, columns(q)], (((1,), (1,)), ((), ())),
            preferred_element_type=jnp.float32,
        )

    @pl.loop(0, pieces)
    def start_far(q):
        for o in far:
            pair(o, q).start()
            keep(o, q).start()

    @pl.loop(0, pieces)
    def start_near(q):
        pair(0, q).start()
        keep(0, q).start()

    for o in [0] + far:
        load(o).start()
    sketch[...] = jnp.zeros_like(sketch)

    @pl.loop(0, pieces)
    def send_far(q):
        for o in far:
            compose(o, q)
            send(o, q).start()

    for o in [0] + far:
        load(o).wait()

    @pl.loop(0, pieces)
    def finish_near(q):
        compose(0, q)
        difference(0, q, mine)

    @pl.loop(0, pieces)
    def finish_far(q):
        for o in far:
            send(o, q).wait_recv()
            difference(o, q, landed)

    @pl.loop(0, pieces)
    def drain(q):
        for o in [0] + far:
            store(o, q).wait()
            pair(o, q).wait_send()
        for o in far:
            send(o, q).wait_send()


def sum_kernel(
    col_count, row_count, partial, full, gram,
    arrived, local_gram, crossed,
    a_send, a_recv, b_send, b_recv, c_send, c_recv, d_send, d_recv,
):
    row = lax.axis_index("row")
    col = lax.axis_index("col")
    own_rows = arrived.shape[1]
    gram_rows = crossed.shape[1]

    def peer(o):
        return lax.rem(col + o, col_count)

    def above(o):
        return lax.rem(row + o, row_count)

    barrier = pltpu.get_barrier_semaphore()
    for o in range(1, col_count):
        pl.semaphore_signal(barrier, inc=1, device_id=(row, peer(o)), device_id_type=MESH)
    for o in range(1, row_count):
        pl.semaphore_signal(barrier, inc=1, device_id=(above(o), col), device_id_type=MESH)
    pl.semaphore_wait(barrier, col_count + row_count - 2)

    own = pl.ds(pl.multiple_of(col * own_rows, own_rows), own_rows)
    strip = pl.ds(pl.multiple_of(col * gram_rows, gram_rows), gram_rows)

    def copy(source, target, send, recv, o, device):
        made = pltpu.make_async_remote_copy(
            src_ref=source, dst_ref=target, send_sem=send.at[o], recv_sem=recv.at[o],
            device_id=device, device_id_type=MESH,
        )
        made.start()
        return made

    first = []
    for o in range(1, col_count):
        theirs = pl.ds(pl.multiple_of(peer(o) * own_rows, own_rows), own_rows)
        first.append(
            copy(partial.at[theirs, :], arrived.at[o], a_send, a_recv, o, (row, peer(o)))
        )
    total = partial[own, :]
    for o in range(1, col_count):
        first[o - 1].wait_recv()
        total = total + arrived[o]
    full[own, :] = total
    second = [
        copy(full.at[own, :], full.at[own, :], b_send, b_recv, o, (row, peer(o)))
        for o in range(1, col_count)
    ]
    for made in second:
        made.wait_recv()
    local_gram[...] = lax.dot_general(
        full[...], full[...], (((0,), (0,)), ((), ())),
        precision=HIGHEST, preferred_element_type=jnp.float32,
    )
    third = [
        copy(local_gram.at[strip, :], crossed.at[o], c_send, c_recv, o, (above(o), col))
        for o in range(1, row_count)
    ]
    total = local_gram[strip, :]
    for o in range(1, row_count):
        third[o - 1].wait_recv()
        total = total + crossed[o]
    gram[strip, :] = total
    fourth = [
        copy(gram.at[strip, :], gram.at[strip, :], d_send, d_recv, o, (row, peer(o)))
        for o in range(1, col_count)
    ]
    for made in fourth:
        made.wait_recv()
    for made in first + second + third + fourth:
        made.wait_send()


def factor_kernel(panel, scale, full, gram, own, narrow, basis, table):
    size = gram.shape[0]
    row_ids = lax.broadcasted_iota(jnp.int32, (size, size), 0)
    column_ids = lax.broadcasted_iota(jnp.int32, (size, size), 1)
    eye = row_ids == column_ids
    diagonal = jnp.where(eye, gram[...], 0.0)
    scale_rows = 1.0 / jnp.sqrt(jnp.sum(diagonal, axis=1, keepdims=True))
    scale_columns = 1.0 / jnp.sqrt(jnp.sum(diagonal, axis=0, keepdims=True))
    table[:, :size] = gram[...] * scale_rows * scale_columns
    table[:, size:] = eye.astype(jnp.float32)
    for start in range(0, size, panel):
        low = start // 128 * 128
        high = size + low + 128
        block = table[start:start + panel, low:high]
        ids = lax.broadcasted_iota(jnp.int32, (panel, 1), 0)
        pivots = jnp.ones((panel, 1), jnp.float32)
        for i in range(0, panel, 2):
            at = start + i - low
            first, second = block[:, at:at + 1], block[:, at + 1:at + 2]
            line, next_line = block[i:i + 1, :], block[i + 1:i + 2, :]
            pivot, cross = first[i:i + 1, :], first[i + 1:i + 2, :]
            determinant = pivot * second[i + 1:i + 2, :] - cross * cross
            inverse_pivot = 1.0 / pivot
            weight = first * inverse_pivot
            next_weight = (second - weight * cross) * (pivot * (1.0 / determinant))
            next_line = next_line - (cross * inverse_pivot) * line
            pivots = jnp.where(ids == i, pivot, pivots)
            pivots = jnp.where(ids == i + 1, determinant * inverse_pivot, pivots)
            block = (
                block
                - jnp.where(ids > i, weight, 0.0) * line
                - jnp.where(ids > i + 1, next_weight, 0.0) * next_line
            )
        block = block * (1.0 / jnp.sqrt(pivots))
        table[start:start + panel, low:high] = block
        end = start + panel
        if end < size:
            update = lax.dot_general(
                block[:, :size - low], block, (((0,), (0,)), ((), ())),
                precision=HIGHEST, preferred_element_type=jnp.float32,
            )
            table[end:, low:high] = table[end:, low:high] - update[end - low:, :]
    inverse = table[:, size:]
    inverse = jnp.where(column_ids <= row_ids, inverse * scale_columns, 0.0)

    turned = lax.dot_general(
        inverse, full[...], (((1,), (1,)), ((), ())),
        precision=HIGHEST, preferred_element_type=jnp.float32,
    )
    narrow[...] = turned.astype(jnp.bfloat16)
    basis[...] = lax.dot_general(
        own[...], inverse, (((1,), (1,)), ((), ())),
        precision=HIGHEST, preferred_element_type=jnp.float32,
    ) * scale


def greet_line(row, row_count, col):
    barrier = pltpu.get_barrier_semaphore()

    @pl.when(row > 0)
    def greet_below():
        pl.semaphore_signal(barrier, inc=1, device_id=(row - 1, col), device_id_type=MESH)

    @pl.when(row < row_count - 1)
    def greet_above():
        pl.semaphore_signal(barrier, inc=1, device_id=(row + 1, col), device_id_type=MESH)

    @pl.when((row > 0) & (row < row_count - 1))
    def hear_both():
        pl.semaphore_wait(barrier, 2)

    @pl.when((row == 0) | (row == row_count - 1))
    def hear_one():
        pl.semaphore_wait(barrier, 1)


def resketch_kernel(
    row_count, narrow, delta, sketch,
    outbox, inbox, result,
    up_send, up_recv, down_send, down_recv,
):
    row = lax.axis_index("row")
    col = lax.axis_index("col")
    pieces, tile = result.shape[0], result.shape[2]
    root = row_count // 2
    side = lax.div(row, root + 1)
    toward = row + 1 - 2 * side
    away = row - 1 + 2 * side
    is_root = row == root
    is_leaf = (row == 0) | ((row == row_count - 1) & (row != root))
    is_middle = jnp.logical_not(is_root | is_leaf)
    root_has_above = root < row_count - 1

    greet_line(row, row_count, col)
    sketch[...] = jnp.zeros_like(sketch)

    def remote(source, target, send, recv, to):
        return pltpu.make_async_remote_copy(
            src_ref=source, dst_ref=target, send_sem=send, recv_sem=recv,
            device_id=(to, col), device_id_type=MESH,
        )

    def inward(t, lane):
        return remote(
            outbox.at[t], inbox.at[lane, t], up_send.at[t], up_recv.at[lane, t], toward
        )

    def outward(t, lane, to):
        return remote(
            result.at[t], result.at[t], down_send.at[lane, t], down_recv.at[t], to
        )

    def gather_piece(t):
        at = pl.ds(pl.multiple_of(t * tile, tile), tile)
        own = jnp.dot(narrow[...], delta[:, at], preferred_element_type=jnp.float32)

        @pl.when(is_leaf)
        def leaf():
            outbox[t] = own.astype(jnp.bfloat16)
            inward(t, side).start()

        @pl.when(is_middle)
        def middle():
            inward(t, side).wait_recv()
            outbox[t] = (own + inbox[side, t].astype(jnp.float32)).astype(jnp.bfloat16)
            inward(t, side).start()

        @pl.when(is_root)
        def centre():
            inward(t, 0).wait_recv()
            total = own + inbox[0, t].astype(jnp.float32)
            if root_has_above:
                inward(t, 1).wait_recv()
                total = total + inbox[1, t].astype(jnp.float32)
            result[t] = total.astype(jnp.bfloat16)
            outward(t, 0, root - 1).start()
            if root_has_above:
                outward(t, 1, root + 1).start()

    def return_piece(t):
        at = pl.ds(pl.multiple_of(t * tile, tile), tile)

        @pl.when(jnp.logical_not(is_root))
        def arrive():
            outward(t, 0, toward).wait_recv()

        @pl.when(is_middle)
        def forward():
            outward(t, 0, away).start()

        sketch[...] += lax.dot_general(
            delta[:, at], result[t], (((1,), (1,)), ((), ())),
            preferred_element_type=jnp.float32,
        )

    lag = jnp.where(is_leaf, pieces, jnp.where(is_root, 0, min(4, pieces)))

    @pl.loop(0, 2 * pieces)
    def run(t):
        @pl.when(t < pieces)
        def ahead():
            gather_piece(t)

        @pl.when((t >= lag) & (t < pieces + lag))
        def behind():
            return_piece(t - lag)

    @pl.loop(0, pieces)
    def drain(t):
        @pl.when(jnp.logical_not(is_root))
        def sent():
            inward(t, side).wait_send()

        @pl.when(jnp.logical_not(is_leaf))
        def returned():
            outward(t, 0, away).wait_send()

        if root_has_above:
            @pl.when(is_root)
            def returned_above():
                outward(t, 1, root + 1).wait_send()


def scatter_kernel(
    row_count, narrow, delta, coefficients,
    own, outbox, inbox, send_sem, recv_sem,
):
    row = lax.axis_index("row")
    col = lax.axis_index("col")
    pieces, block, tile = outbox.shape[2], outbox.shape[3], outbox.shape[4]
    near = lax.div(2 * row, row_count)

    greet_line(row, row_count, col)

    def columns(t):
        return pl.ds(pl.multiple_of(t * tile, 128), tile)

    def rows(index):
        return pl.ds(pl.multiple_of(index * block, block), block)

    def move(way, index, t, to):
        return pltpu.make_async_remote_copy(
            src_ref=outbox.at[way, index, t], dst_ref=inbox.at[way, index, t],
            send_sem=send_sem.at[way, index, t], recv_sem=recv_sem.at[way, index, t],
            device_id=(to, col), device_id_type=MESH,
        )

    def flow(way, t):
        behind = row + way * (row_count - 1 - 2 * row)
        ahead = row_count - 1 - behind
        source, target = row - 1 + 2 * way, row + 1 - 2 * way
        for k in range(row_count - 1, 0, -1):
            index = row + k * (1 - 2 * way)

            @pl.when((k <= ahead) & (behind > 0))
            def relay():
                move(way, index, t, source).wait_recv()
                total = own[rows(index), columns(t)] + inbox[way, index, t].astype(jnp.float32)
                outbox[way, index, t] = total.astype(jnp.bfloat16)
                move(way, index, t, target).start()

            @pl.when((k <= ahead) & (behind == 0))
            def begin():
                outbox[way, index, t] = own[rows(index), columns(t)].astype(jnp.bfloat16)
                move(way, index, t, target).start()

        @pl.when(behind > 0)
        def finish():
            move(way, row, t, source).wait_recv()
            own[rows(row), columns(t)] += inbox[way, row, t].astype(jnp.float32)

    is_leaf = (row == 0) | (row == row_count - 1)
    lag = jnp.where(is_leaf, pieces, min(3, pieces))

    @pl.loop(0, 2 * pieces)
    def run(t):
        @pl.when(t < pieces)
        def first():
            own[:, columns(t)] = jnp.dot(
                narrow[...], delta[:, columns(t)], preferred_element_type=jnp.float32
            )
            flow(near, t)

        @pl.when((t >= lag) & (t < pieces + lag))
        def second():
            flow(1 - near, t - lag)
            coefficients[:, columns(t - lag)] = own[rows(row), columns(t - lag)]

    @pl.loop(0, pieces)
    def drain(t):
        for way in range(2):
            ahead = row if way else row_count - 1 - row
            for k in range(1, row_count):
                @pl.when(k <= ahead)
                def sent():
                    move(way, row + k * (1 - 2 * way), t, row + 1 - 2 * way).wait_send()


def vmem():
    return pl.BlockSpec(memory_space=pltpu.VMEM)


def anywhere():
    return pl.BlockSpec(memory_space=pl.ANY)


def gather(select, base_rows, finetune, test_matrix, chips):
    capacity = base_rows.shape[0]
    rows, width = finetune.shape
    sketch_size = test_matrix.shape[0]
    slots = pltpu.VMEM((chips, capacity, width), jnp.bfloat16)
    lanes = width // 128
    pieces = lanes // max(d for d in range(1, 17) if lanes % d == 0)
    each = pltpu.SemaphoreType.DMA((chips, pieces))
    block = pltpu.SemaphoreType.DMA((chips,))
    return pl.pallas_call(
        functools.partial(gather_kernel, chips),
        out_shape=(
            jax.ShapeDtypeStruct((rows, width), jnp.bfloat16),
            jax.ShapeDtypeStruct((rows, sketch_size), jnp.float32),
        ),
        in_specs=[vmem(), anywhere(), anywhere(), vmem()],
        out_specs=(anywhere(), vmem()),
        scratch_shapes=[slots] * 4 + [each] * 5 + [block, each],
        compiler_params=pltpu.CompilerParams(
            collective_id=0, has_side_effects=True, vmem_limit_bytes=VMEM_LIMIT
        ),
        cost_estimate=pl.CostEstimate(
            flops=2 * rows * width * sketch_size, bytes_accessed=8 * rows * width, transcendentals=0
        ),
    )(select, base_rows, finetune, test_matrix)


def group_sums(partial, col_count, row_count, collective_id):
    rows, size = partial.shape
    col_sems = pltpu.SemaphoreType.DMA((col_count,))
    row_sems = pltpu.SemaphoreType.DMA((row_count,))
    return pl.pallas_call(
        functools.partial(sum_kernel, col_count, row_count),
        out_shape=(
            jax.ShapeDtypeStruct((rows, size), jnp.float32),
            jax.ShapeDtypeStruct((size, size), jnp.float32),
        ),
        in_specs=[vmem()],
        out_specs=(vmem(), vmem()),
        scratch_shapes=[
            pltpu.VMEM((col_count, rows // col_count, size), jnp.float32),
            pltpu.VMEM((size, size), jnp.float32),
            pltpu.VMEM((row_count, size // col_count, size), jnp.float32),
            col_sems, col_sems, col_sems, col_sems,
            row_sems, row_sems, col_sems, col_sems,
        ],
        compiler_params=pltpu.CompilerParams(
            collective_id=collective_id, has_side_effects=True, vmem_limit_bytes=VMEM_LIMIT
        ),
    )(partial)


def orthonormal(full, gram, own, scale):
    rows, size = full.shape
    return pl.pallas_call(
        functools.partial(factor_kernel, 32, scale),
        out_shape=(
            jax.ShapeDtypeStruct((size, rows), jnp.bfloat16),
            jax.ShapeDtypeStruct(own.shape, jnp.float32),
        ),
        in_specs=[vmem()] * 3,
        out_specs=(vmem(), vmem()),
        scratch_shapes=[pltpu.VMEM((size, 2 * size), jnp.float32)],
        compiler_params=pltpu.CompilerParams(vmem_limit_bytes=VMEM_LIMIT),
    )(full, gram, own)


def resketch(narrow, delta, row_count):
    rows, width = delta.shape
    size = narrow.shape[0]
    tile = 256 if width % 256 == 0 else 128
    pieces = width // tile
    one = pltpu.SemaphoreType.DMA((pieces,))
    two = pltpu.SemaphoreType.DMA((2, pieces))
    return pl.pallas_call(
        functools.partial(resketch_kernel, row_count),
        out_shape=jax.ShapeDtypeStruct((rows, size), jnp.float32),
        in_specs=[vmem()] * 2,
        out_specs=vmem(),
        scratch_shapes=[
            pltpu.VMEM((pieces, size, tile), jnp.bfloat16),
            pltpu.VMEM((2, pieces, size, tile), jnp.bfloat16),
            pltpu.VMEM((pieces, size, tile), jnp.bfloat16),
            one, two, two, one,
        ],
        compiler_params=pltpu.CompilerParams(
            collective_id=3, has_side_effects=True, vmem_limit_bytes=VMEM_LIMIT
        ),
    )(narrow, delta)


def scatter(narrow, delta, row_count):
    rows, width = delta.shape
    size = narrow.shape[0]
    block = size // row_count
    tile = column_tile(width)
    pieces = width // tile
    box = pltpu.VMEM((2, row_count, pieces, block, tile), jnp.bfloat16)
    sems = pltpu.SemaphoreType.DMA((2, row_count, pieces))
    return pl.pallas_call(
        functools.partial(scatter_kernel, row_count),
        out_shape=jax.ShapeDtypeStruct((block, width), jnp.float32),
        in_specs=[vmem()] * 2,
        out_specs=vmem(),
        scratch_shapes=[pltpu.VMEM((size, width), jnp.float32), box, box, sems, sems],
        compiler_params=pltpu.CompilerParams(
            collective_id=4, has_side_effects=True, vmem_limit_bytes=VMEM_LIMIT
        ),
    )(narrow, delta)


def per_device(finetune, base_rows, test_matrix, base_lengths):
    col_count = lax.axis_size("col")
    row_count = lax.axis_size("row")
    col = lax.axis_index("col")
    row = lax.axis_index("row")
    capacity = base_rows.shape[0]
    chips = col_count // 2
    group = finetune.shape[0]
    total_rows = group * row_count
    own_rows = group // col_count

    first_count = lax.dynamic_index_in_dim(
        base_lengths, row * col_count + col // 2 * 2, 0, keepdims=False
    )
    slab_row = jnp.arange(capacity)[:, None]
    slot = jnp.arange(capacity)[None, :]
    from_first = (slab_row == slot) & (slab_row < first_count)
    from_second = slab_row - first_count == slot
    is_first = col % 2 == 0
    select = jnp.stack(
        [jnp.where(is_first, from_first, from_second), jnp.where(is_first, from_second, from_first)]
    ).astype(jnp.bfloat16)

    delta, partial = gather(select, base_rows, finetune, test_matrix, chips)
    for sweep in range(2):
        full, gram = group_sums(partial, col_count, row_count, 1 + sweep)
        own = lax.dynamic_slice_in_dim(full, col * own_rows, own_rows, 0)
        narrow, basis = orthonormal(full, gram, own, math.sqrt(total_rows))
        if sweep == 0:
            partial = resketch(narrow, delta, row_count)
    coefficients = scatter(narrow, delta, row_count)
    return (basis, coefficients)


def solution(mesh):
    return jax.shard_map(
        per_device,
        mesh=mesh,
        in_specs=(P("row", "col"), P(("row", "col"), None), P(None, "col"), P()),
        out_specs=(P(("row", "col"), None), P("row", "col")),
        check_vma=False,
    )
```

```python
import functools
import math

import jax
import jax.numpy as jnp
from jax import lax
from jax.experimental import pallas as pl
from jax.experimental.pallas import tpu as pltpu
from jax.sharding import PartitionSpec as P

MESH = pl.DeviceIdType.MESH
HIGHEST = lax.Precision.HIGHEST
VMEM_LIMIT = 58 * 1024 * 1024


def flip(index, mask, count):
    if count & (count - 1):
        raise ValueError("count")
    result, bit = 0, 1
    while bit < count:
        digit = lax.rem(lax.div(index, bit), 2)
        result = result + bit * ((1 - digit) if mask & bit else digit)
        bit *= 2
    return result


def column_tile(width):
    lanes = width // 128
    return 128 * max(d for d in range(1, 9) if lanes % d == 0)


def gather_kernel(
    chips, select, base, fine, test, delta, sketch,
    mine, other, landed, work,
    mine_sem, pair_send, pair_recv, send_sem, recv_sem, fine_sem, delta_sem,
):
    row = lax.axis_index("row")
    col = lax.axis_index("col")
    chip = lax.div(col, 2)
    core = lax.rem(col, 2)
    rows, width = mine.shape[1], mine.shape[2]
    pieces = mine_sem.shape[1]
    tile = width // pieces
    partner = (row, 2 * chip + (1 - core))

    barrier = pltpu.get_barrier_semaphore()
    pl.semaphore_signal(barrier, inc=1, device_id=partner, device_id_type=MESH)
    for o in range(1, chips):
        pl.semaphore_signal(
            barrier, inc=1, device_id=(row, 2 * flip(chip, o, chips) + core), device_id_type=MESH
        )
    pl.semaphore_wait(barrier, chips)

    far = list(range(chips - 1, 0, -1))

    def columns(q):
        return pl.ds(pl.multiple_of(q * tile, 128), tile)

    def rows_of(o):
        return pl.ds(pl.multiple_of(flip(chip, o, chips) * rows, rows), rows)

    def source(o, q, side):
        start = (2 * flip(chip, o, chips) + side) * width + q * tile
        return base.at[:, pl.ds(pl.multiple_of(start, 128), tile)]

    def pair(o, q):
        return pltpu.make_async_remote_copy(
            src_ref=source(o, q, 1 - core), dst_ref=other.at[o, :, columns(q)],
            send_sem=pair_send.at[o, q], recv_sem=pair_recv.at[o, q],
            device_id=partner, device_id_type=MESH,
        )

    def keep(o, q):
        return pltpu.make_async_copy(
            source(o, q, core), mine.at[o, :, columns(q)], mine_sem.at[o, q]
        )

    def load(o):
        return pltpu.make_async_copy(fine.at[rows_of(o), :], work.at[o], fine_sem.at[o])

    def send(o, q):
        return pltpu.make_async_remote_copy(
            src_ref=mine.at[o, :, columns(q)], dst_ref=landed.at[o, :, columns(q)],
            send_sem=send_sem.at[o, q], recv_sem=recv_sem.at[o, q],
            device_id=(row, 2 * flip(chip, o, chips) + core), device_id_type=MESH,
        )

    def store(o, q):
        return pltpu.make_async_copy(
            work.at[o, :, columns(q)], delta.at[rows_of(o), columns(q)], delta_sem.at[o, q]
        )

    def compose(o, q):
        keep(o, q).wait()
        pair(o, q).wait_recv()
        merged = jnp.dot(
            select[0], mine[o, :, columns(q)], preferred_element_type=jnp.float32
        ) + jnp.dot(
            select[1], other[o, :, columns(q)], preferred_element_type=jnp.float32
        )
        mine[o, :, columns(q)] = merged.astype(jnp.bfloat16)

    def difference(o, q, composed):
        value = work[o, :, columns(q)].astype(jnp.float32)
        value = (value - composed[o, :, columns(q)].astype(jnp.float32)).astype(jnp.bfloat16)
        work[o, :, columns(q)] = value
        store(o, q).start()
        sketch[rows_of(o), :] += lax.dot_general(
            value, test[:, columns(q)], (((1,), (1,)), ((), ())),
            preferred_element_type=jnp.float32,
        )

    @pl.loop(0, pieces)
    def start_far(q):
        for o in far:
            pair(o, q).start()
            keep(o, q).start()

    @pl.loop(0, pieces)
    def start_near(q):
        pair(0, q).start()
        keep(0, q).start()

    for o in [0] + far:
        load(o).start()
    sketch[...] = jnp.zeros_like(sketch)

    @pl.loop(0, pieces)
    def send_far(q):
        for o in far:
            compose(o, q)
            send(o, q).start()

    for o in [0] + far:
        load(o).wait()

    @pl.loop(0, pieces)
    def finish_near(q):
        compose(0, q)
        difference(0, q, mine)

    @pl.loop(0, pieces)
    def finish_far(q):
        for o in far:
            send(o, q).wait_recv()
            difference(o, q, landed)

    @pl.loop(0, pieces)
    def drain(q):
        for o in [0] + far:
            store(o, q).wait()
            pair(o, q).wait_send()
        for o in far:
            send(o, q).wait_send()


def sum_kernel(
    col_count, row_count, partial, full, gram, own_sum,
    arrived, local_gram, crossed,
    a_send, a_recv, b_send, b_recv, c_send, c_recv, d_send, d_recv,
):
    row = lax.axis_index("row")
    col = lax.axis_index("col")
    own_rows = arrived.shape[1]
    gram_rows = crossed.shape[1]

    def peer(o):
        return lax.rem(col + o, col_count)

    def above(o):
        return lax.rem(row + o, row_count)

    barrier = pltpu.get_barrier_semaphore()
    for o in range(1, col_count):
        pl.semaphore_signal(barrier, inc=1, device_id=(row, peer(o)), device_id_type=MESH)
    for o in range(1, row_count):
        pl.semaphore_signal(barrier, inc=1, device_id=(above(o), col), device_id_type=MESH)
    pl.semaphore_wait(barrier, col_count + row_count - 2)

    own = pl.ds(pl.multiple_of(col * own_rows, own_rows), own_rows)
    strip = pl.ds(pl.multiple_of(col * gram_rows, gram_rows), gram_rows)

    def copy(source, target, send, recv, o, device):
        made = pltpu.make_async_remote_copy(
            src_ref=source, dst_ref=target, send_sem=send.at[o], recv_sem=recv.at[o],
            device_id=device, device_id_type=MESH,
        )
        made.start()
        return made

    first = []
    for o in range(1, col_count):
        theirs = pl.ds(pl.multiple_of(peer(o) * own_rows, own_rows), own_rows)
        first.append(
            copy(partial.at[theirs, :], arrived.at[o], a_send, a_recv, o, (row, peer(o)))
        )
    total = partial[own, :]
    for o in range(1, col_count):
        first[o - 1].wait_recv()
        total = total + arrived[o]
    full[own, :] = total
    own_sum[...] = total
    second = [
        copy(full.at[own, :], full.at[own, :], b_send, b_recv, o, (row, peer(o)))
        for o in range(1, col_count)
    ]
    for made in second:
        made.wait_recv()
    local_gram[...] = lax.dot_general(
        full[...], full[...], (((0,), (0,)), ((), ())),
        precision=HIGHEST, preferred_element_type=jnp.float32,
    )
    third = [
        copy(local_gram.at[strip, :], crossed.at[o], c_send, c_recv, o, (above(o), col))
        for o in range(1, row_count)
    ]
    total = local_gram[strip, :]
    for o in range(1, row_count):
        third[o - 1].wait_recv()
        total = total + crossed[o]
    gram[strip, :] = total
    fourth = [
        copy(gram.at[strip, :], gram.at[strip, :], d_send, d_recv, o, (row, peer(o)))
        for o in range(1, col_count)
    ]
    for made in fourth:
        made.wait_recv()
    for made in first + second + third + fourth:
        made.wait_send()


def factor_kernel(panel, scale, full, gram, own, narrow, basis, table):
    size = gram.shape[0]
    row_ids = lax.broadcasted_iota(jnp.int32, (size, size), 0)
    column_ids = lax.broadcasted_iota(jnp.int32, (size, size), 1)
    table[:, :size] = gram[...]
    table[:, size:] = (row_ids == column_ids).astype(jnp.float32)
    for start in range(0, size, panel):
        low = start // 128 * 128
        high = size + low + 128
        block = table[start:start + panel, low:high]
        ids = lax.broadcasted_iota(jnp.int32, (panel, 1), 0)
        pivots = jnp.ones((panel, 1), jnp.float32)
        for i in range(panel):
            at = start + i - low
            column = block[:, at:at + 1]
            line = block[i:i + 1, :]
            pivot = column[i:i + 1, :]
            pivots = jnp.where(ids == i, pivot, pivots)
            if i + 1 < panel:
                weight = jnp.where(ids > i, column * (1.0 / pivot), 0.0)
                block = block - weight * line
        block = block * (1.0 / jnp.sqrt(pivots))
        table[start:start + panel, low:high] = block
        end = start + panel
        if end < size:
            update = lax.dot_general(
                block[:, :size - low], block, (((0,), (0,)), ((), ())),
                precision=HIGHEST, preferred_element_type=jnp.float32,
            )
            table[end:, low:high] = table[end:, low:high] - update[end - low:, :]
    inverse = table[:, size:]
    inverse = jnp.where(column_ids <= row_ids, inverse, 0.0)

    turned = lax.dot_general(
        inverse, full[...], (((1,), (1,)), ((), ())),
        precision=HIGHEST, preferred_element_type=jnp.float32,
    )
    narrow[...] = turned.astype(jnp.bfloat16)
    basis[...] = lax.dot_general(
        own[...], inverse, (((1,), (1,)), ((), ())),
        precision=HIGHEST, preferred_element_type=jnp.float32,
    ) * scale


def greet_line(row, row_count, col):
    barrier = pltpu.get_barrier_semaphore()

    @pl.when(row > 0)
    def greet_below():
        pl.semaphore_signal(barrier, inc=1, device_id=(row - 1, col), device_id_type=MESH)

    @pl.when(row < row_count - 1)
    def greet_above():
        pl.semaphore_signal(barrier, inc=1, device_id=(row + 1, col), device_id_type=MESH)

    @pl.when((row > 0) & (row < row_count - 1))
    def hear_both():
        pl.semaphore_wait(barrier, 2)

    @pl.when((row == 0) | (row == row_count - 1))
    def hear_one():
        pl.semaphore_wait(barrier, 1)


def resketch_kernel(
    row_count, narrow, delta, sketch,
    outbox, inbox, result,
    up_send, up_recv, down_send, down_recv,
):
    row = lax.axis_index("row")
    col = lax.axis_index("col")
    pieces, tile = result.shape[0], result.shape[2]
    root = row_count // 2
    side = lax.div(row, root + 1)
    toward = row + 1 - 2 * side
    away = row - 1 + 2 * side
    is_root = row == root
    is_leaf = (row == 0) | ((row == row_count - 1) & (row != root))
    is_middle = jnp.logical_not(is_root | is_leaf)
    root_has_above = root < row_count - 1

    greet_line(row, row_count, col)
    sketch[...] = jnp.zeros_like(sketch)

    def remote(source, target, send, recv, to):
        return pltpu.make_async_remote_copy(
            src_ref=source, dst_ref=target, send_sem=send, recv_sem=recv,
            device_id=(to, col), device_id_type=MESH,
        )

    def inward(t, lane):
        return remote(
            outbox.at[t], inbox.at[lane, t], up_send.at[t], up_recv.at[lane, t], toward
        )

    def outward(t, lane, to):
        return remote(
            result.at[t], result.at[t], down_send.at[lane, t], down_recv.at[t], to
        )

    def gather_piece(t):
        at = pl.ds(pl.multiple_of(t * tile, tile), tile)
        own = jnp.dot(narrow[...], delta[:, at], preferred_element_type=jnp.float32)

        @pl.when(is_leaf)
        def leaf():
            outbox[t] = own.astype(jnp.bfloat16)
            inward(t, side).start()

        @pl.when(is_middle)
        def middle():
            inward(t, side).wait_recv()
            outbox[t] = (own + inbox[side, t].astype(jnp.float32)).astype(jnp.bfloat16)
            inward(t, side).start()

        @pl.when(is_root)
        def centre():
            inward(t, 0).wait_recv()
            total = own + inbox[0, t].astype(jnp.float32)
            if root_has_above:
                inward(t, 1).wait_recv()
                total = total + inbox[1, t].astype(jnp.float32)
            result[t] = total.astype(jnp.bfloat16)
            outward(t, 0, root - 1).start()
            if root_has_above:
                outward(t, 1, root + 1).start()

    def return_piece(t):
        at = pl.ds(pl.multiple_of(t * tile, tile), tile)

        @pl.when(jnp.logical_not(is_root))
        def arrive():
            outward(t, 0, toward).wait_recv()

        @pl.when(is_middle)
        def forward():
            outward(t, 0, away).start()

        sketch[...] += lax.dot_general(
            delta[:, at], result[t], (((1,), (1,)), ((), ())),
            preferred_element_type=jnp.float32,
        )

    lag = jnp.where(is_leaf, pieces, jnp.where(is_root, 0, min(4, pieces)))

    @pl.loop(0, 2 * pieces)
    def run(t):
        @pl.when(t < pieces)
        def ahead():
            gather_piece(t)

        @pl.when((t >= lag) & (t < pieces + lag))
        def behind():
            return_piece(t - lag)

    @pl.loop(0, pieces)
    def drain(t):
        @pl.when(jnp.logical_not(is_root))
        def sent():
            inward(t, side).wait_send()

        @pl.when(jnp.logical_not(is_leaf))
        def returned():
            outward(t, 0, away).wait_send()

        if root_has_above:
            @pl.when(is_root)
            def returned_above():
                outward(t, 1, root + 1).wait_send()


def scatter_kernel(
    row_count, narrow, delta, coefficients,
    own, outbox, inbox, send_sem, recv_sem,
):
    row = lax.axis_index("row")
    col = lax.axis_index("col")
    pieces, block, tile = outbox.shape[2], outbox.shape[3], outbox.shape[4]
    near = lax.div(2 * row, row_count)

    greet_line(row, row_count, col)

    def columns(t):
        return pl.ds(pl.multiple_of(t * tile, 128), tile)

    def rows(index):
        return pl.ds(pl.multiple_of(index * block, block), block)

    def move(way, index, t, to):
        return pltpu.make_async_remote_copy(
            src_ref=outbox.at[way, index, t], dst_ref=inbox.at[way, index, t],
            send_sem=send_sem.at[way, index, t], recv_sem=recv_sem.at[way, index, t],
            device_id=(to, col), device_id_type=MESH,
        )

    def flow(way, t):
        behind = row + way * (row_count - 1 - 2 * row)
        ahead = row_count - 1 - behind
        source, target = row - 1 + 2 * way, row + 1 - 2 * way
        for k in range(row_count - 1, 0, -1):
            index = row + k * (1 - 2 * way)

            @pl.when((k <= ahead) & (behind > 0))
            def relay():
                move(way, index, t, source).wait_recv()
                total = own[rows(index), columns(t)] + inbox[way, index, t].astype(jnp.float32)
                outbox[way, index, t] = total.astype(jnp.bfloat16)
                move(way, index, t, target).start()

            @pl.when((k <= ahead) & (behind == 0))
            def begin():
                outbox[way, index, t] = own[rows(index), columns(t)].astype(jnp.bfloat16)
                move(way, index, t, target).start()

        @pl.when(behind > 0)
        def finish():
            move(way, row, t, source).wait_recv()
            own[rows(row), columns(t)] += inbox[way, row, t].astype(jnp.float32)

    is_leaf = (row == 0) | (row == row_count - 1)
    lag = jnp.where(is_leaf, pieces, min(3, pieces))

    @pl.loop(0, 2 * pieces)
    def run(t):
        @pl.when(t < pieces)
        def first():
            own[:, columns(t)] = jnp.dot(
                narrow[...], delta[:, columns(t)], preferred_element_type=jnp.float32
            )
            flow(near, t)

        @pl.when((t >= lag) & (t < pieces + lag))
        def second():
            flow(1 - near, t - lag)
            coefficients[:, columns(t - lag)] = own[rows(row), columns(t - lag)]

    @pl.loop(0, pieces)
    def drain(t):
        for way in range(2):
            ahead = row if way else row_count - 1 - row
            for k in range(1, row_count):
                @pl.when(k <= ahead)
                def sent():
                    move(way, row + k * (1 - 2 * way), t, row + 1 - 2 * way).wait_send()


def vmem():
    return pl.BlockSpec(memory_space=pltpu.VMEM)


def anywhere():
    return pl.BlockSpec(memory_space=pl.ANY)


def gather(select, base_rows, finetune, test_matrix, chips):
    capacity = base_rows.shape[0]
    rows, width = finetune.shape
    sketch_size = test_matrix.shape[0]
    slots = pltpu.VMEM((chips, capacity, width), jnp.bfloat16)
    lanes = width // 128
    pieces = lanes // max(d for d in range(1, 17) if lanes % d == 0)
    each = pltpu.SemaphoreType.DMA((chips, pieces))
    block = pltpu.SemaphoreType.DMA((chips,))
    return pl.pallas_call(
        functools.partial(gather_kernel, chips),
        out_shape=(
            jax.ShapeDtypeStruct((rows, width), jnp.bfloat16),
            jax.ShapeDtypeStruct((rows, sketch_size), jnp.float32),
        ),
        in_specs=[vmem(), anywhere(), anywhere(), vmem()],
        out_specs=(anywhere(), vmem()),
        scratch_shapes=[slots] * 4 + [each] * 5 + [block, each],
        compiler_params=pltpu.CompilerParams(
            collective_id=0, has_side_effects=True, vmem_limit_bytes=VMEM_LIMIT
        ),
        cost_estimate=pl.CostEstimate(
            flops=2 * rows * width * sketch_size, bytes_accessed=8 * rows * width, transcendentals=0
        ),
    )(select, base_rows, finetune, test_matrix)


def group_sums(partial, col_count, row_count, collective_id):
    rows, size = partial.shape
    col_sems = pltpu.SemaphoreType.DMA((col_count,))
    row_sems = pltpu.SemaphoreType.DMA((row_count,))
    return pl.pallas_call(
        functools.partial(sum_kernel, col_count, row_count),
        out_shape=(
            jax.ShapeDtypeStruct((rows, size), jnp.float32),
            jax.ShapeDtypeStruct((size, size), jnp.float32),
            jax.ShapeDtypeStruct((rows // col_count, size), jnp.float32),
        ),
        in_specs=[vmem()],
        out_specs=(vmem(), vmem(), vmem()),
        scratch_shapes=[
            pltpu.VMEM((col_count, rows // col_count, size), jnp.float32),
            pltpu.VMEM((size, size), jnp.float32),
            pltpu.VMEM((row_count, size // col_count, size), jnp.float32),
            col_sems, col_sems, col_sems, col_sems,
            row_sems, row_sems, col_sems, col_sems,
        ],
        compiler_params=pltpu.CompilerParams(
            collective_id=collective_id, has_side_effects=True, vmem_limit_bytes=VMEM_LIMIT
        ),
    )(partial)


def orthonormal(full, gram, own, scale):
    rows, size = full.shape
    return pl.pallas_call(
        functools.partial(factor_kernel, 32, scale),
        out_shape=(
            jax.ShapeDtypeStruct((size, rows), jnp.bfloat16),
            jax.ShapeDtypeStruct(own.shape, jnp.float32),
        ),
        in_specs=[vmem()] * 3,
        out_specs=(vmem(), vmem()),
        scratch_shapes=[pltpu.VMEM((size, 2 * size), jnp.float32)],
        compiler_params=pltpu.CompilerParams(vmem_limit_bytes=VMEM_LIMIT),
    )(full, gram, own)


def resketch(narrow, delta, row_count):
    rows, width = delta.shape
    size = narrow.shape[0]
    tile = 256 if width % 256 == 0 else 128
    pieces = width // tile
    one = pltpu.SemaphoreType.DMA((pieces,))
    two = pltpu.SemaphoreType.DMA((2, pieces))
    return pl.pallas_call(
        functools.partial(resketch_kernel, row_count),
        out_shape=jax.ShapeDtypeStruct((rows, size), jnp.float32),
        in_specs=[vmem()] * 2,
        out_specs=vmem(),
        scratch_shapes=[
            pltpu.VMEM((pieces, size, tile), jnp.bfloat16),
            pltpu.VMEM((2, pieces, size, tile), jnp.bfloat16),
            pltpu.VMEM((pieces, size, tile), jnp.bfloat16),
            one, two, two, one,
        ],
        compiler_params=pltpu.CompilerParams(
            collective_id=3, has_side_effects=True, vmem_limit_bytes=VMEM_LIMIT
        ),
    )(narrow, delta)


def scatter(narrow, delta, row_count):
    rows, width = delta.shape
    size = narrow.shape[0]
    block = size // row_count
    tile = column_tile(width)
    pieces = width // tile
    box = pltpu.VMEM((2, row_count, pieces, block, tile), jnp.bfloat16)
    sems = pltpu.SemaphoreType.DMA((2, row_count, pieces))
    return pl.pallas_call(
        functools.partial(scatter_kernel, row_count),
        out_shape=jax.ShapeDtypeStruct((block, width), jnp.float32),
        in_specs=[vmem()] * 2,
        out_specs=vmem(),
        scratch_shapes=[pltpu.VMEM((size, width), jnp.float32), box, box, sems, sems],
        compiler_params=pltpu.CompilerParams(
            collective_id=4, has_side_effects=True, vmem_limit_bytes=VMEM_LIMIT
        ),
    )(narrow, delta)


def per_device(finetune, base_rows, test_matrix, base_lengths):
    col_count = lax.axis_size("col")
    row_count = lax.axis_size("row")
    col = lax.axis_index("col")
    row = lax.axis_index("row")
    capacity = base_rows.shape[0]
    chips = col_count // 2
    group = finetune.shape[0]
    total_rows = group * row_count

    first_count = lax.dynamic_index_in_dim(
        base_lengths, row * col_count + col // 2 * 2, 0, keepdims=False
    )
    slab_row = jnp.arange(capacity)[:, None]
    slot = jnp.arange(capacity)[None, :]
    from_first = (slab_row == slot) & (slab_row < first_count)
    from_second = slab_row - first_count == slot
    is_first = col % 2 == 0
    select = jnp.stack(
        [jnp.where(is_first, from_first, from_second), jnp.where(is_first, from_second, from_first)]
    ).astype(jnp.bfloat16)

    delta, partial = gather(select, base_rows, finetune, test_matrix, chips)
    for sweep in range(2):
        full, gram, own = group_sums(partial, col_count, row_count, 1 + sweep)
        narrow, basis = orthonormal(full, gram, own, math.sqrt(total_rows))
        if sweep == 0:
            partial = resketch(narrow, delta, row_count)
    coefficients = scatter(narrow, delta, row_count)
    return (basis, coefficients)


def solution(mesh):
    return jax.shard_map(
        per_device,
        mesh=mesh,
        in_specs=(P("row", "col"), P(("row", "col"), None), P(None, "col"), P()),
        out_specs=(P(("row", "col"), None), P("row", "col")),
        check_vma=False,
    )
```
